256 devices in a mesh: cgrp: 8 (over z), dev: 32 (over x, y, core).
Axes of the slice: x: 4, y: 4, z: 8, core: 2. Of those that a mesh axis runs over, the one named last changes fastest.
Arguments:
- docs: bfloat16 [65536, 1024], P('dev'), may hold values from -140 to 140
- centroids: float32 [8192, 1024], P(('cgrp', 'dev')), may hold values from -6 to 6
Outputs:
- centroids_next: float32 [8192, 1024], P(('cgrp', 'dev'))
- mass: float32 [8192], P(('cgrp', 'dev'))
- doc_lse: float32 [65536], P('dev')
The draws below stay inside these ranges and needn't reach their ends.
All inputs are finite; a program needn't handle non-finite values.
Results may differ from the reference program's by a relative error of at most 0.012.
The reference program's roundings to bfloat16 on the way (of `rounded`) count: a program that leaves them out, or rounds other values in their place, can miss the bound.
Values may be sent and summed in bfloat16 or wider, within the bound.
A program may use at most 64 MiB of HBM per device.

```python
import math
import jax
import jax.numpy as jnp
from jax import lax

D = 1024
DOCS = 65536
K = 8192


def centroid_table(key):
    first_key = jax.random.fold_in(key, 11)
    return jnp.clip(jax.random.normal(first_key, (K, D)), -6.0, 6.0).astype(jnp.float32)


def draw_centroids(key, part):
    return centroid_table(key)


def draw_docs(key, part):
    table = centroid_table(key)
    key = jax.random.fold_in(key, 5)
    base = jnp.clip(jax.random.normal(jax.random.fold_in(key, 23), (DOCS, D)), -6.0, 6.0)
    first = jax.random.randint(jax.random.fold_in(key, 31), (DOCS,), 0, K)
    second = (first + jax.random.randint(jax.random.fold_in(key, 37), (DOCS,), 1, K)) % K
    levels = jnp.array([210.0, 260.0, 320.0], jnp.float32)
    target = levels[jax.random.randint(jax.random.fold_in(key, 41), (DOCS,), 0, 3)]
    strength = 0.5 + target / (4.0 * math.sqrt(D))
    beta = 4.0 / math.sqrt(D)
    delta = 2.0 / (beta * strength * D)
    aligned = strength[:, None] * (table[first] + (1.0 + delta)[:, None] * table[second])
    chosen = jnp.arange(DOCS) % 8 == 0
    base = jnp.where(chosen[:, None], aligned, base)
    return jnp.clip(base, -140.0, 140.0).astype(jnp.float32).astype(jnp.bfloat16)


def setup_inputs(seed: int = 0) -> dict:
    streams_of = jax.random.split(jax.random.key(seed), 3)
    docs = draw_docs(jax.random.fold_in(streams_of[2], 71), 0)
    centroids = draw_centroids(jax.random.fold_in(streams_of[2], 71), 0)
    return dict(docs=docs, centroids=centroids)


def block_scores(docs, cent_block):
    scale = 4.0 / math.sqrt(docs.shape[1])
    rounded = cent_block.astype(jnp.bfloat16)
    wide = rounded.astype(jnp.float32)
    norms = lax.optimization_barrier(jnp.sum(wide * wide, axis=1))
    dots = jnp.dot(docs, rounded.T, preferred_element_type=jnp.float32)
    return (dots - 0.5 * norms[None, :]) * scale

def reference(docs, centroids):
    width = 2048 if K >= 2048 else K
    blocks = centroids.reshape(K // width, width, D)
    docs_wide = docs.astype(jnp.float32)

    def stat_step(carry, cent_block):
        run_max, run_sum = carry
        scores = block_scores(docs, cent_block)
        new_max = jnp.maximum(run_max, lax.optimization_barrier(jnp.max(scores, axis=1)))
        run_sum = run_sum * jnp.exp(run_max - new_max) + lax.optimization_barrier(jnp.sum(jnp.exp(scores - new_max[:, None]), axis=1))
        return ((new_max, run_sum), None)
    start = (jnp.full((DOCS,), -1e+30, jnp.float32), jnp.zeros((DOCS,), jnp.float32))
    (run_max, run_sum), unused = lax.scan(stat_step, start, blocks)
    doc_lse = run_max + jnp.log(run_sum)

    def update(cent_block):
        scores = block_scores(docs, cent_block)
        resp = jnp.exp(scores - doc_lse[:, None])
        mass = lax.optimization_barrier(jnp.sum(resp, axis=0))
        weighted = jnp.dot(resp.T, docs_wide, preferred_element_type=jnp.float32, precision=lax.Precision.HIGHEST)
        return ((weighted + cent_block) / (mass[:, None] + 1.0), mass)
    new_blocks, masses = lax.map(update, blocks)
    return (new_blocks.reshape(K, D), masses.reshape(K), doc_lse)
```

```python
import jax
import jax.numpy as jnp
from jax import lax
from jax.experimental import pallas as pl
from jax.experimental.pallas import tpu as pltpu
from jax.sharding import PartitionSpec as P

MESH = pl.DeviceIdType.MESH
WIDTH = 1024
DOCS = 2048
ROWS = 32
HALF = 128
WIDE = WIDTH + 128
SCALE = 0.125
TILE = 256


def em_kernel(
    docs_hbm, cent_ref, acc_ref, lse_ref,
    docs, mine, sib, expo, top, total, lses, factor,
    keep, out_sib, in_sib, out_v, in_v, out_a, in_a,
    docs_sem, s1, r1, s2, r2, s3, r3, s4, r4, s5, r5, s6, r6, s7, r7,
):
    z = lax.axis_index("cgrp")
    dev = lax.axis_index("dev")
    core = lax.rem(dev, 2)
    x = lax.div(dev, 8)
    y = lax.rem(lax.div(dev, 2), 4)
    a = x * (1 - core) + y * core
    v = y * (1 - core) + x * core

    def rot(p, k):
        return lax.rem(p + (k + 4), 4)

    def at(ai, vi):
        xi = ai * (1 - core) + vi * core
        yi = vi * (1 - core) + ai * core
        return (z, (xi * 4 + yi) * 2 + core)

    sibling = (z, dev + 1 - 2 * core)

    def up(k):
        return (lax.rem(z + k, 8), dev)

    def rows(i):
        return pl.ds(pl.multiple_of(i * ROWS, ROWS), ROWS)

    def remote(src, dst, send, recv, where):
        return pltpu.make_async_remote_copy(
            src_ref=src, dst_ref=dst, send_sem=send, recv_sem=recv, device_id=where, device_id_type=MESH
        )

    load = pltpu.make_async_copy(docs_hbm, docs, docs_sem)
    load.start()
    barrier = pltpu.get_barrier_semaphore()
    greet = [at(a, rot(v, k)) for k in (1, 2, 3)] + [at(rot(a, k), v) for k in (1, 2, 3)]
    greet += [sibling] + [up(k) for k in range(1, 8)]
    for where in greet:
        pl.semaphore_signal(barrier, inc=1, device_id=where, device_id_type=MESH)
    mine[a, rows(v)] = cent_ref[...].astype(jnp.bfloat16)
    pl.semaphore_wait(barrier, len(greet))

    def block(da, dj):
        return mine.at[rot(a, -da), rows(rot(v, -dj))]

    def along_v(dv):
        return remote(block(0, 0), block(0, 0), s1.at[dv], r1.at[dv], at(a, rot(v, dv)))

    def arrived_v(dv):
        return remote(block(0, dv), block(0, dv), s1.at[dv], r1.at[dv], at(a, rot(v, dv)))

    def along_a(da, dj):
        return remote(block(0, dj), block(0, dj), s2.at[da, dj], r2.at[da, dj], at(rot(a, da), v))

    def arrived_a(da, dj):
        return remote(block(da, dj), block(da, dj), s2.at[da, dj], r2.at[da, dj], at(rot(a, da), v))

    def across(da, dj):
        where = sib.at[rot(a, -da), rows(rot(v, -dj))]
        return remote(block(da, dj), where, s3.at[da, dj], r3.at[da, dj], sibling)

    def arrived_across(da, dj):
        where = sib.at[rot(v, -da), rows(rot(a, -dj))]
        return remote(where, where, s3.at[da, dj], r3.at[da, dj], sibling)

    def scores(t):
        for dj in (0, 1, 3, 2):
            arrived_across(t, dj).wait_recv()
        cent = jnp.concatenate([mine[rot(a, -t)], sib[rot(v, -t)]], axis=0)
        wide = cent.astype(jnp.float32)
        bias = jnp.sum(wide * wide, axis=1, keepdims=True) * (0.5 * SCALE)
        for i in range(DOCS // TILE):
            part = pl.ds(i * TILE, TILE)
            dots = lax.dot_general(
                cent, docs[part, :], (((1,), (1,)), ((), ())), preferred_element_type=jnp.float32
            )
            s = dots * SCALE - bias
            m = jnp.max(s, axis=0, keepdims=True)
            p = jnp.exp(s - m)
            expo[t, :, part] = p.astype(jnp.bfloat16)
            top[t, :, part] = m
            total[t, :, part] = jnp.sum(p, axis=0, keepdims=True)

    for dv in (1, 3, 2):
        along_v(dv).start()
    for da in (1, 3, 2):
        along_a(da, 0).start()
    across(0, 0).start()
    for dv in (1, 3, 2):
        arrived_v(dv).wait_recv()
        for da in (1, 3, 2):
            along_a(da, dv).start()
        across(0, dv).start()
    load.wait()
    scores(0)
    for da in (1, 3):
        for dj in (0, 1, 3, 2):
            arrived_a(da, dj).wait_recv()
            across(da, dj).start()
    scores(1)
    for dj in (0, 1):
        arrived_a(2, dj).wait_recv()
        across(2, dj).start()
    scores(3)
    for dj in (3, 2):
        arrived_a(2, dj).wait_recv()
        across(2, dj).start()
    scores(2)

    m = jnp.maximum(jnp.maximum(top[0], top[1]), jnp.maximum(top[2], top[3]))
    l = sum(total[t] * jnp.exp(top[t] - m) for t in range(4))
    lses[z] = m + jnp.log(l)

    def along_z(k):
        return remote(lses.at[z], lses.at[z], s4.at[k], r4.at[k], up(k))

    def arrived_z(k):
        where = lses.at[lax.rem(z + 8 - k, 8)]
        return remote(where, where, s4.at[k], r4.at[k], up(k))

    for k in (4, 3, 5, 2, 6, 1, 7):
        along_z(k).start()
    for k in (1, 7, 2, 6, 3, 5, 4):
        arrived_z(k).wait_recv()
    m = lses[0]
    for k in range(1, 8):
        m = jnp.maximum(m, lses[k])
    lse = m + jnp.log(sum(jnp.exp(lses[k] - m) for k in range(8)))
    lse_ref[...] = lse
    for t in range(4):
        factor[t] = jnp.exp(top[t] - lse)

    def give(t):
        return remote(out_sib.at[t], in_sib.at[t], s5.at[t], r5.at[t], sibling)

    def sum_v(t, dv):
        return remote(
            out_v.at[t, rows(rot(v, dv))], in_v.at[t, dv - 1], s6.at[t, dv], r6.at[t, dv], at(a, rot(v, dv))
        )

    def sum_a(t):
        return remote(out_a.at[t - 1], in_a.at[t - 1], s7.at[t], r7.at[t], at(rot(a, -t), v))

    def weigh(t):
        resp = expo[t].astype(jnp.float32) * factor[t]
        mass = jnp.broadcast_to(jnp.sum(resp, axis=1, keepdims=True), (2 * HALF, 128))
        keep[t, :, pl.ds(WIDTH, 128)] = mass[:HALF]
        out_sib[t, :, pl.ds(WIDTH, 128)] = mass[HALF:].astype(jnp.bfloat16)
        resp = resp.astype(jnp.bfloat16)
        for j in range(WIDTH // TILE):
            part = pl.ds(j * TILE, TILE)
            term = jnp.dot(resp, docs[:, part], preferred_element_type=jnp.float32)
            keep[t, :, part] = term[:HALF]
            out_sib[t, :, part] = term[HALF:].astype(jnp.bfloat16)
        give(t).start()

    def pair(t):
        give(t).wait_recv()
        both = keep[t] + in_sib[t].astype(jnp.float32)
        keep[t] = both
        out_v[t] = both.astype(jnp.bfloat16)
        for dv in (2, 1, 3):
            sum_v(t, dv).start()

    def row(t):
        for dv in (1, 3, 2):
            sum_v(t, dv).wait_recv()
        own = keep[t, rows(v)]
        for dv in (1, 2, 3):
            own = own + in_v[t, dv - 1].astype(jnp.float32)
        if t == 0:
            return own
        out_a[t - 1] = own.astype(jnp.bfloat16)
        sum_a(t).start()

    weigh(2)
    weigh(1)
    pair(2)
    weigh(3)
    pair(1)
    weigh(0)
    pair(3)
    pair(0)
    row(2)
    row(1)
    row(3)
    acc = row(0)
    for t in (1, 3, 2):
        sum_a(t).wait_recv()
        acc = acc + in_a[t - 1].astype(jnp.float32)
    acc_ref[...] = acc

    for dv in (1, 2, 3):
        along_v(dv).wait_send()
    for da in (1, 2, 3):
        for dj in range(4):
            along_a(da, dj).wait_send()
    for da in range(4):
        for dj in range(4):
            across(da, dj).wait_send()
    for k in range(1, 8):
        along_z(k).wait_send()
    for t in range(4):
        give(t).wait_send()
        for dv in (1, 2, 3):
            sum_v(t, dv).wait_send()
        if t:
            sum_a(t).wait_send()


def finish_kernel(acc_ref, lse_in, cent_ref, next_ref, mass_ref, lse_ref):
    mass = acc_ref[:, pl.ds(WIDTH, 128)]
    next_ref[...] = (acc_ref[:, pl.ds(0, WIDTH)] + cent_ref[...]) / (mass[:, :1] + 1.0)
    mass_ref[...] = jnp.transpose(mass)[0]
    lse_ref[...] = lse_in[0]


def body(docs, centroids):
    bf16, f32 = jnp.bfloat16, jnp.float32
    dma = pltpu.SemaphoreType.DMA
    vmem = pl.BlockSpec(memory_space=pltpu.VMEM)
    acc, lse = pl.pallas_call(
        em_kernel,
        out_shape=(jax.ShapeDtypeStruct((ROWS, WIDE), f32), jax.ShapeDtypeStruct((1, DOCS), f32)),
        in_specs=[pl.BlockSpec(memory_space=pl.ANY), vmem],
        out_specs=(vmem, vmem),
        scratch_shapes=[
            pltpu.VMEM((DOCS, WIDTH), bf16),
            pltpu.VMEM((4, HALF, WIDTH), bf16),
            pltpu.VMEM((4, HALF, WIDTH), bf16),
            pltpu.VMEM((4, 2 * HALF, DOCS), bf16),
            pltpu.VMEM((4, 1, DOCS), f32),
            pltpu.VMEM((4, 1, DOCS), f32),
            pltpu.VMEM((8, 1, DOCS), f32),
            pltpu.VMEM((4, 1, DOCS), f32),
            pltpu.VMEM((4, HALF, WIDE), f32),
            pltpu.VMEM((4, HALF, WIDE), bf16),
            pltpu.VMEM((4, HALF, WIDE), bf16),
            pltpu.VMEM((4, HALF, WIDE), bf16),
            pltpu.VMEM((4, 3, ROWS, WIDE), bf16),
            pltpu.VMEM((3, ROWS, WIDE), bf16),
            pltpu.VMEM((3, ROWS, WIDE), bf16),
            dma,
            dma((4,)), dma((4,)),
            dma((4, 4)), dma((4, 4)),
            dma((4, 4)), dma((4, 4)),
            dma((8,)), dma((8,)),
            dma((4,)), dma((4,)),
            dma((4, 4)), dma((4, 4)),
            dma((4,)), dma((4,)),
        ],
        compiler_params=pltpu.CompilerParams(
            collective_id=0, has_side_effects=True, vmem_limit_bytes=56 * 2**20
        ),
        cost_estimate=pl.CostEstimate(
            flops=4 * DOCS * WIDTH * 1024, bytes_accessed=2 * DOCS * WIDTH, transcendentals=DOCS * 1024
        ),
        name="em_step",
    )(docs, centroids)
    return pl.pallas_call(
        finish_kernel,
        out_shape=(
            jax.ShapeDtypeStruct((ROWS, WIDTH), f32),
            jax.ShapeDtypeStruct((ROWS,), f32),
            jax.ShapeDtypeStruct((DOCS,), f32),
        ),
        in_specs=[vmem] * 3,
        out_specs=(vmem,) * 3,
        name="finish",
    )(acc, lse, centroids)


def solution(mesh):
    in_specs = (P("dev", None), P(("cgrp", "dev"), None))
    out_specs = (P(("cgrp", "dev"), None), P(("cgrp", "dev")), P("dev"))
    return jax.shard_map(body, mesh=mesh, in_specs=in_specs, out_specs=out_specs, check_vma=False)
```

```python
import jax
import jax.numpy as jnp
from jax import lax
from jax.experimental import pallas as pl
from jax.experimental.pallas import tpu as pltpu
from jax.sharding import PartitionSpec as P

MESH = pl.DeviceIdType.MESH
WIDTH = 1024
DOCS = 2048
ROWS = 32
HALF = 128
WIDE = WIDTH + 128
SCALE = 0.125
TILE = 256
GROUPS = 10


def em_kernel(
    docs_hbm, cent_hbm, acc_ref, lse_ref,
    docs, turned, cent, mine, sib, expo, top, total, lses, factor,
    keep, out_sib, in_sib, out_v, in_v, out_a, in_a,
    docs_sem, cent_sem, low_sem, high_sem,
    s1, r1, s2, r2, s3, r3, s4, r4, s5, r5, s6, r6, s7, r7,
):
    z = lax.axis_index("cgrp")
    dev = lax.axis_index("dev")
    core = lax.rem(dev, 2)
    x = lax.div(dev, 8)
    y = lax.rem(lax.div(dev, 2), 4)
    a = x * (1 - core) + y * core
    v = y * (1 - core) + x * core

    def at(da, dv):
        ai = lax.rem(a + (da + 4), 4)
        vi = lax.rem(v + (dv + 4), 4)
        xi = ai * (1 - core) + vi * core
        yi = vi * (1 - core) + ai * core
        return (z, (xi * 4 + yi) * 2 + core)

    sibling = (z, dev + 1 - 2 * core)

    def up(k):
        return (lax.rem(z + k, 8), dev)

    def rows(i, n=1):
        return pl.ds(i * ROWS, n * ROWS)

    def remote(src, dst, send, recv, where):
        return pltpu.make_async_remote_copy(
            src_ref=src, dst_ref=dst, send_sem=send, recv_sem=recv, device_id=where, device_id_type=MESH
        )

    def signal(sem, where):
        pl.semaphore_signal(sem, inc=1, device_id=where, device_id_type=MESH)

    barrier = pltpu.get_barrier_semaphore()
    greet = [at(0, 2), at(2, 0), at(0, 1), at(0, 3), at(1, 0), at(3, 0), sibling, up(1), up(7)]
    own = pltpu.make_async_copy(cent_hbm, cent, cent_sem)
    own.start()
    for where in greet:
        signal(barrier, where)
    load = pltpu.make_async_copy(docs_hbm, docs, docs_sem)
    load.start()
    own.wait()
    mine[0, rows(0)] = cent[...].astype(jnp.bfloat16)
    pl.semaphore_wait(barrier, len(greet))

    def tell_low():
        signal(low_sem, up(1))

    def tell_high():
        signal(high_sem, up(7))

    def told():
        pl.semaphore_wait(low_sem, 1)
        pl.semaphore_wait(high_sem, 1)

    def along_v(dv):
        return remote(mine.at[0, rows(0)], mine.at[0, rows(dv)], s1.at[dv], r1.at[dv], at(0, dv))

    def along_a(da, dj):
        return remote(mine.at[0, rows(dj)], mine.at[da, rows(dj)], s2.at[da, dj], r2.at[da, dj], at(da, 0))

    def across(da, dj):
        return remote(mine.at[da, rows(dj)], sib.at[da, rows(dj)], s3.at[da, dj], r3.at[da, dj], sibling)

    def scores(g, blocks):
        c = jnp.concatenate([b[t, rows(j, n)] for b, t, j, n, _ in blocks], axis=0)
        wide = c.astype(jnp.float32)
        bias = jnp.sum(wide * wide, axis=1, keepdims=True) * (0.5 * SCALE)
        for i in range(DOCS // TILE):
            part = pl.ds(i * TILE, TILE)
            dots = jnp.dot(c, turned[:, part], preferred_element_type=jnp.float32)
            s = dots * SCALE - bias
            m = jnp.max(s, axis=0, keepdims=True)
            p = jnp.exp(s - m)
            e = p.astype(jnp.bfloat16)
            done = 0
            for _, t, _, n, r in blocks:
                expo[t, rows(r, n), part] = e[done * ROWS:(done + n) * ROWS]
                done += n
            top[pl.ds(g, 1), part] = m
            total[pl.ds(g, 1), part] = jnp.sum(p, axis=0, keepdims=True)

    def from_mine(dj):
        return [(mine, da, dj, 1, dj) for da in (1, 2, 3)]

    def from_sib(dj):
        return [(sib, da, dj, 1, dj + 4) for da in (1, 2, 3)]

    def forward_a(dj):
        for da in (1, 3, 2):
            along_a(da, dj).wait_recv()
            across(da, dj).start()

    def wait_across(dj):
        for da in (1, 3, 2):
            across(da, dj).wait_recv()

    for dv in (1, 3, 2):
        along_v(dv).start()
    for da in (1, 3, 2):
        along_a(da, 0).start()
    across(0, 0).start()
    tell_low()
    tell_high()
    load.wait()
    for i in range(DOCS // TILE):
        part = pl.ds(i * TILE, TILE)
        turned[:, part] = jnp.transpose(docs[part, :])
    for dv in (1, 3, 2):
        along_v(dv).wait_recv()
        for da in (1, 3, 2):
            along_a(da, dv).start()
        across(0, dv).start()
    forward_a(0)
    told()
    tell_low()
    tell_high()
    scores(0, [(mine, 0, 0, 4, 0)])
    scores(1, from_mine(0))
    for dj in (0, 1, 3, 2):
        across(0, dj).wait_recv()
    scores(2, [(sib, 0, 0, 4, 4)])
    told()
    tell_low()
    wait_across(0)
    scores(3, from_sib(0))
    forward_a(1)
    scores(4, from_mine(1))
    forward_a(3)
    wait_across(1)
    scores(5, from_sib(1))
    scores(6, from_mine(3))
    forward_a(2)
    wait_across(3)
    scores(7, from_sib(3))
    scores(8, from_mine(2))
    wait_across(2)
    scores(9, from_sib(2))

    tops = top[...]
    m = jnp.max(tops, axis=0, keepdims=True)
    l = jnp.sum(total[...] * jnp.exp(tops - m), axis=0, keepdims=True)
    lses[z] = m + jnp.log(l)

    def along_z(k):
        return remote(lses.at[z], lses.at[z], s4.at[k], r4.at[k], up(k))

    def arrived_z(k):
        where = lses.at[lax.rem(z + 8 - k, 8)]
        return remote(where, where, s4.at[k], r4.at[k], up(k))

    pl.semaphore_wait(low_sem, 1)
    for k in (4, 3, 5, 2, 6, 1, 7):
        along_z(k).start()
    for k in (1, 7, 2, 6, 3, 5, 4):
        arrived_z(k).wait_recv()
    m = lses[0]
    for k in range(1, 8):
        m = jnp.maximum(m, lses[k])
    lse = m + jnp.log(sum(jnp.exp(lses[k] - m) for k in range(8)))
    lse_ref[...] = lse
    factor[...] = jnp.exp(tops - lse)

    def give(t):
        return remote(out_sib.at[t], in_sib.at[t], s5.at[t], r5.at[t], sibling)

    def sum_v(t, dv):
        return remote(
            out_v.at[t, rows(4 - dv)], in_v.at[t, dv - 1], s6.at[t, dv], r6.at[t, dv], at(0, dv)
        )

    def sum_a(t):
        return remote(out_a.at[t - 1], in_a.at[t - 1], s7.at[t], r7.at[t], at(-t, 0))

    def weigh(t, other, out):
        parts = [
            expo[t, rows(4 * other + dj)].astype(jnp.float32) * factor[pl.ds(first + step * other, 1), :]
            for dj, (first, step) in enumerate([(0, 2)] * 4 if t == 0 else [(1, 2), (4, 1), (8, 1), (6, 1)])
        ]
        resp = jnp.concatenate(parts, axis=0)
        mass = jnp.broadcast_to(jnp.sum(resp, axis=1, keepdims=True), (HALF, 128))
        out[t, :, pl.ds(WIDTH, 128)] = mass.astype(out.dtype)
        resp = resp.astype(jnp.bfloat16)
        for j in range(WIDTH // TILE):
            part = pl.ds(j * TILE, TILE)
            term = jnp.dot(resp, docs[:, part], preferred_element_type=jnp.float32)
            out[t, :, part] = term.astype(out.dtype)

    def theirs(t):
        weigh(t, 1, out_sib)
        give(t).start()

    def ours(t):
        weigh(t, 0, keep)

    def pair(t):
        give(t).wait_recv()
        both = keep[t] + in_sib[t].astype(jnp.float32)
        keep[t] = both
        out_v[t] = both.astype(jnp.bfloat16)
        for dv in (2, 1, 3):
            sum_v(t, dv).start()

    def row(t):
        for dv in (1, 3, 2):
            sum_v(t, dv).wait_recv()
        own = keep[t, rows(0)]
        for dv in (1, 2, 3):
            own = own + in_v[t, dv - 1].astype(jnp.float32)
        if t == 0:
            return own
        out_a[t - 1] = own.astype(jnp.bfloat16)
        sum_a(t).start()

    theirs(2)
    ours(2)
    theirs(1)
    pair(2)
    ours(1)
    theirs(3)
    pair(1)
    ours(3)
    theirs(0)
    pair(3)
    ours(0)
    pair(0)
    row(2)
    row(1)
    row(3)
    acc = row(0)
    for t in (1, 3, 2):
        sum_a(t).wait_recv()
        acc = acc + in_a[t - 1].astype(jnp.float32)
    acc_ref[...] = acc

    for dv in (1, 2, 3):
        along_v(dv).wait_send()
    for da in (1, 2, 3):
        for dj in range(4):
            along_a(da, dj).wait_send()
    for da in range(4):
        for dj in range(4):
            across(da, dj).wait_send()
    for k in range(1, 8):
        along_z(k).wait_send()
    for t in range(4):
        give(t).wait_send()
        for dv in (1, 2, 3):
            sum_v(t, dv).wait_send()
        if t:
            sum_a(t).wait_send()


def finish_kernel(acc_ref, lse_in, cent_ref, next_ref, mass_ref, lse_ref):
    mass = acc_ref[:, pl.ds(WIDTH, 128)]
    next_ref[...] = (acc_ref[:, pl.ds(0, WIDTH)] + cent_ref[...]) / (mass[:, :1] + 1.0)
    mass_ref[...] = jnp.transpose(mass)[0]
    lse_ref[...] = lse_in[0]


def body(docs, centroids):
    bf16, f32 = jnp.bfloat16, jnp.float32
    dma = pltpu.SemaphoreType.DMA
    flag = pltpu.SemaphoreType.REGULAR
    vmem = pl.BlockSpec(memory_space=pltpu.VMEM)
    acc, lse = pl.pallas_call(
        em_kernel,
        out_shape=(jax.ShapeDtypeStruct((ROWS, WIDE), f32), jax.ShapeDtypeStruct((1, DOCS), f32)),
        in_specs=[pl.BlockSpec(memory_space=pl.ANY)] * 2,
        out_specs=(vmem, vmem),
        scratch_shapes=[
            pltpu.VMEM((DOCS, WIDTH), bf16),
            pltpu.VMEM((WIDTH, DOCS), bf16),
            pltpu.VMEM((ROWS, WIDTH), f32),
            pltpu.VMEM((4, HALF, WIDTH), bf16),
            pltpu.VMEM((4, HALF, WIDTH), bf16),
            pltpu.VMEM((4, 2 * HALF, DOCS), bf16),
            pltpu.VMEM((GROUPS, DOCS), f32),
            pltpu.VMEM((GROUPS, DOCS), f32),
            pltpu.VMEM((8, 1, DOCS), f32),
            pltpu.VMEM((GROUPS, DOCS), f32),
            pltpu.VMEM((4, HALF, WIDE), f32),
            pltpu.VMEM((4, HALF, WIDE), bf16),
            pltpu.VMEM((4, HALF, WIDE), bf16),
            pltpu.VMEM((4, HALF, WIDE), bf16),
            pltpu.VMEM((4, 3, ROWS, WIDE), bf16),
            pltpu.VMEM((3, ROWS, WIDE), bf16),
            pltpu.VMEM((3, ROWS, WIDE), bf16),
            dma, dma, flag, flag,
            dma((4,)), dma((4,)),
            dma((4, 4)), dma((4, 4)),
            dma((4, 4)), dma((4, 4)),
            dma((8,)), dma((8,)),
            dma((4,)), dma((4,)),
            dma((4, 4)), dma((4, 4)),
            dma((4,)), dma((4,)),
        ],
        compiler_params=pltpu.CompilerParams(
            collective_id=0, has_side_effects=True, vmem_limit_bytes=56 * 2**20
        ),
        cost_estimate=pl.CostEstimate(
            flops=4 * DOCS * WIDTH * 1024, bytes_accessed=2 * DOCS * WIDTH, transcendentals=DOCS * 1024
        ),
        name="em_step",
    )(docs, centroids)
    return pl.pallas_call(
        finish_kernel,
        out_shape=(
            jax.ShapeDtypeStruct((ROWS, WIDTH), f32),
            jax.ShapeDtypeStruct((ROWS,), f32),
            jax.ShapeDtypeStruct((DOCS,), f32),
        ),
        in_specs=[vmem] * 3,
        out_specs=(vmem,) * 3,
        name="finish",
    )(acc, lse, centroids)


def solution(mesh):
    in_specs = (P("dev", None), P(("cgrp", "dev"), None))
    out_specs = (P(("cgrp", "dev"), None), P(("cgrp", "dev")), P("dev"))
    return jax.shard_map(body, mesh=mesh, in_specs=in_specs, out_specs=out_specs, check_vma=False)
```

```python
import jax
import jax.numpy as jnp
from jax import lax
from jax.experimental import pallas as pl
from jax.experimental.pallas import tpu as pltpu
from jax.sharding import PartitionSpec as P

MESH = pl.DeviceIdType.MESH
WIDTH = 1024
DOCS = 2048
ROWS = 32
HALF = 128
WIDE = WIDTH + 128
TALL = ROWS * WIDTH // 128 + 16
SCALE = 0.125
TILE = 256
GROUPS = 10


def em_kernel(
    docs_hbm, cent_hbm, acc_ref, lse_ref,
    docs, turned, cent, mine, sib, expo, top, total, lses, factor,
    keep, keep_own, out_sib, in_sib, out_v, in_v, out_a, in_a,
    docs_sem, cent_sem, low_sem, high_sem,
    s1, r1, s2, r2, s3, r3, s4, r4, s5, r5, s6, r6, s7, r7,
):
    z = lax.axis_index("cgrp")
    dev = lax.axis_index("dev")
    core = lax.rem(dev, 2)
    x = lax.div(dev, 8)
    y = lax.rem(lax.div(dev, 2), 4)
    a = x * (1 - core) + y * core
    v = y * (1 - core) + x * core

    def at(da, dv):
        ai = lax.rem(a + (da + 4), 4)
        vi = lax.rem(v + (dv + 4), 4)
        xi = ai * (1 - core) + vi * core
        yi = vi * (1 - core) + ai * core
        return (z, (xi * 4 + yi) * 2 + core)

    sibling = (z, dev + 1 - 2 * core)

    def up(k):
        return (lax.rem(z + k, 8), dev)

    def rows(i, n=1):
        return pl.ds(i * ROWS, n * ROWS)

    def remote(src, dst, send, recv, where):
        return pltpu.make_async_remote_copy(
            src_ref=src, dst_ref=dst, send_sem=send, recv_sem=recv, device_id=where, device_id_type=MESH
        )

    def signal(sem, where):
        pl.semaphore_signal(sem, inc=1, device_id=where, device_id_type=MESH)

    barrier = pltpu.get_barrier_semaphore()
    greet = [at(0, 2), at(2, 0), at(0, 1), at(0, 3), at(1, 0), at(3, 0), sibling, up(1), up(7)]
    own = pltpu.make_async_copy(cent_hbm, cent, cent_sem)
    own.start()
    for where in greet:
        signal(barrier, where)
    load = pltpu.make_async_copy(docs_hbm, docs, docs_sem)
    load.start()
    own.wait()
    mine[0, rows(0)] = cent[...].astype(jnp.bfloat16)
    pl.semaphore_wait(barrier, len(greet))

    def tell_low():
        signal(low_sem, up(1))

    def tell_high():
        signal(high_sem, up(7))

    def told():
        pl.semaphore_wait(low_sem, 1)
        pl.semaphore_wait(high_sem, 1)

    def along_v(dv):
        return remote(mine.at[0, rows(0)], mine.at[0, rows(dv)], s1.at[dv], r1.at[dv], at(0, dv))

    def along_a(da, dj):
        return remote(mine.at[0, rows(dj)], mine.at[da, rows(dj)], s2.at[da, dj], r2.at[da, dj], at(da, 0))

    def across(da, dj):
        return remote(mine.at[da, rows(dj)], sib.at[da, rows(dj)], s3.at[da, dj], r3.at[da, dj], sibling)

    def scores(g, blocks):
        c = jnp.concatenate([b[t, rows(j, n)] for b, t, j, n, _ in blocks], axis=0)
        wide = c.astype(jnp.float32)
        bias = jnp.sum(wide * wide, axis=1, keepdims=True) * (0.5 * SCALE)
        for i in range(DOCS // TILE):
            part = pl.ds(i * TILE, TILE)
            dots = jnp.dot(c, turned[:, part], preferred_element_type=jnp.float32)
            s = dots * SCALE - bias
            m = jnp.max(s, axis=0, keepdims=True)
            p = jnp.exp(s - m)
            e = p.astype(jnp.bfloat16)
            done = 0
            for _, t, _, n, r in blocks:
                expo[t, rows(r, n), part] = e[done * ROWS:(done + n) * ROWS]
                done += n
            top[pl.ds(g, 1), part] = m
            total[pl.ds(g, 1), part] = jnp.sum(p, axis=0, keepdims=True)

    def from_mine(dj):
        return [(mine, da, dj, 1, dj) for da in (1, 2, 3)]

    def from_sib(dj):
        return [(sib, da, dj, 1, dj + 4) for da in (1, 2, 3)]

    def forward_a(dj):
        for da in (1, 3, 2):
            along_a(da, dj).wait_recv()
            across(da, dj).start()

    def wait_across(dj):
        for da in (1, 3, 2):
            across(da, dj).wait_recv()

    def turn(tiles):
        for i in tiles:
            part = pl.ds(i * TILE, TILE)
            turned[:, part] = jnp.transpose(docs[part, :])

    for k in (1, 3, 2):
        along_v(k).start()
    across(0, 0).start()
    tell_low()
    tell_high()
    for k in (1, 3, 2):
        along_a(k, 0).start()
    load.wait()
    turn(range(8))
    for dv in (1, 3, 2):
        along_v(dv).wait_recv()
        for da in (1, 3, 2):
            along_a(da, dv).start()
        across(0, dv).start()
    forward_a(0)
    told()
    tell_low()
    tell_high()
    scores(0, [(mine, 0, 0, 4, 0)])
    scores(1, from_mine(0))
    for dj in (0, 1, 3, 2):
        across(0, dj).wait_recv()
    scores(2, [(sib, 0, 0, 4, 4)])
    told()
    tell_low()
    wait_across(0)
    scores(3, from_sib(0))
    forward_a(1)
    scores(4, from_mine(1))
    forward_a(3)
    wait_across(1)
    scores(5, from_sib(1))
    scores(6, from_mine(3))
    forward_a(2)
    wait_across(3)
    scores(7, from_sib(3))
    scores(8, from_mine(2))
    wait_across(2)
    scores(9, from_sib(2))

    tops = top[...]
    m = jnp.max(tops, axis=0, keepdims=True)
    l = jnp.sum(total[...] * jnp.exp(tops - m), axis=0, keepdims=True)
    lses[z] = m + jnp.log(l)

    def along_z(k):
        return remote(lses.at[z], lses.at[z], s4.at[k], r4.at[k], up(k))

    def arrived_z(k):
        where = lses.at[lax.rem(z + 8 - k, 8)]
        return remote(where, where, s4.at[k], r4.at[k], up(k))

    pl.semaphore_wait(low_sem, 1)
    for k in (4, 3, 5, 2, 6, 1, 7):
        along_z(k).start()
    for dv in (1, 2, 3):
        along_v(dv).wait_send()
    for da in (1, 2, 3):
        for dj in range(4):
            along_a(da, dj).wait_send()
    for da in range(4):
        for dj in range(4):
            across(da, dj).wait_send()
    for k in (1, 7, 2, 6, 3, 5, 4):
        arrived_z(k).wait_recv()
    m = lses[0]
    for k in range(1, 8):
        m = jnp.maximum(m, lses[k])
    lse = m + jnp.log(sum(jnp.exp(lses[k] - m) for k in range(8)))
    lse_ref[...] = lse
    factor[...] = jnp.exp(tops - lse)

    whole = {t: [(t, 0, WIDE, 0, TALL)] for t in (0, 1, 3)}
    pieces = {2: [(4, 0, WIDTH // 2, 0, TALL // 2 - 8), (2, WIDTH // 2, WIDE - WIDTH // 2, TALL // 2 - 8, TALL // 2 + 8)]}
    pieces.update(whole)

    def give(t, piece):
        sem, col, n, _, _ = piece
        part = pl.ds(col, n)
        return remote(out_sib.at[t, :, part], in_sib.at[t, :, part], s5.at[sem], r5.at[sem], sibling)

    def sum_v(t, piece, dv):
        sem, _, _, first, n = piece
        part = pl.ds(first, n)
        return remote(
            out_v.at[t, 4 - dv, part], in_v.at[t, dv - 1, part], s6.at[sem, dv], r6.at[sem, dv], at(0, dv)
        )

    def sum_a(t):
        return remote(out_a.at[t - 1], in_a.at[t - 1], s7.at[t], r7.at[t], at(-t, 0))

    left = lax.broadcasted_iota(jnp.int32, (16, 128), 1) < 64

    def emit(t, col, both):
        for dj in (2, 3, 1, 0):
            block = both[dj * ROWS:(dj + 1) * ROWS]
            out = keep_own if dj == 0 else out_v
            for j in range(0, both.shape[1], 128):
                values = block[:, j:j + 128]
                if col + j == WIDTH:
                    values = jnp.where(left, values[:16], values[16:])
                lines = pl.ds((col + j) // 128 * ROWS, values.shape[0])
                out[t, dj, lines, :] = values.astype(out.dtype)

    def weigh(t, other, save, done):
        parts = [
            expo[t, rows(4 * other + dj)].astype(jnp.float32) * factor[pl.ds(first + step * other, 1), :]
            for dj, (first, step) in enumerate([(0, 2)] * 4 if t == 0 else [(1, 2), (4, 1), (8, 1), (6, 1)])
        ]
        resp = jnp.concatenate(parts, axis=0)
        mass = jnp.sum(resp, axis=1, keepdims=True)
        resp = resp.astype(jnp.bfloat16)
        for piece in pieces[t]:
            _, col, n, _, _ = piece
            for j in range(col, col + n, TILE):
                if j == WIDTH:
                    save(j, jnp.broadcast_to(mass, (HALF, 128)))
                else:
                    save(j, jnp.dot(resp, docs[:, pl.ds(j, TILE)], preferred_element_type=jnp.float32))
            done(piece)

    def theirs(t):
        def save(j, term):
            out_sib[t, :, pl.ds(j, term.shape[1])] = term.astype(jnp.bfloat16)

        weigh(t, 1, save, lambda piece: give(t, piece).start())

    def send_v(t, piece):
        for dv in (2, 1, 3):
            sum_v(t, piece, dv).start()

    def ours(t):
        for piece in pieces[t]:
            give(t, piece).wait_recv()

        def save(j, term):
            emit(t, j, term + in_sib[t, :, pl.ds(j, term.shape[1])].astype(jnp.float32))

        weigh(t, 0, save, lambda piece: send_v(t, piece))

    def ours_first(t):
        def save(j, term):
            keep[:, pl.ds(j, term.shape[1])] = term

        weigh(t, 0, save, lambda piece: None)
        for piece in pieces[t]:
            _, col, n, _, _ = piece
            give(t, piece).wait_recv()
            emit(t, col, keep[:, pl.ds(col, n)] + in_sib[t, :, pl.ds(col, n)].astype(jnp.float32))
            send_v(t, piece)

    def row(t):
        for piece in pieces[t]:
            for dv in (1, 3, 2):
                sum_v(t, piece, dv).wait_recv()
        own = keep_own[t, 0]
        for dv in (1, 2, 3):
            own = own + in_v[t, dv - 1].astype(jnp.float32)
        if t == 0:
            return own
        out_a[t - 1] = own.astype(jnp.bfloat16)
        sum_a(t).start()

    theirs(2)
    theirs(1)
    ours_first(2)
    theirs(3)
    ours(1)
    theirs(0)
    ours(3)
    ours(0)
    for k in range(1, 8):
        along_z(k).wait_send()
    for t in range(4):
        for piece in pieces[t]:
            give(t, piece).wait_send()
    row(2)
    row(1)
    row(3)
    for t in (2, 1, 3):
        for dv in (1, 2, 3):
            for piece in pieces[t]:
                sum_v(t, piece, dv).wait_send()
    acc = row(0)
    for t in (1, 3, 2):
        sum_a(t).wait_recv()
        acc = acc + in_a[t - 1].astype(jnp.float32)
    acc_ref[...] = acc

    for t in (1, 2, 3):
        sum_a(t).wait_send()
    for dv in (1, 2, 3):
        sum_v(0, pieces[0][0], dv).wait_send()


def finish_kernel(acc_ref, lse_in, cent_ref, next_ref, mass_ref, lse_ref):
    packed = acc_ref[pl.ds(WIDTH // 128 * ROWS, 16), :]
    mass = jnp.concatenate([packed[:, :1], packed[:, 64:65]], axis=0)
    for j in range(WIDTH // 128):
        part = pl.ds(j * 128, 128)
        next_ref[:, part] = (acc_ref[pl.ds(j * ROWS, ROWS), :] + cent_ref[:, part]) / (mass + 1.0)
    mass_ref[...] = jnp.transpose(jnp.broadcast_to(mass, (ROWS, 128)))[0]
    lse_ref[...] = lse_in[0]


def body(docs, centroids):
    bf16, f32 = jnp.bfloat16, jnp.float32
    dma = pltpu.SemaphoreType.DMA
    flag = pltpu.SemaphoreType.REGULAR
    vmem = pl.BlockSpec(memory_space=pltpu.VMEM)
    acc, lse = pl.pallas_call(
        em_kernel,
        out_shape=(jax.ShapeDtypeStruct((TALL, 128), f32), jax.ShapeDtypeStruct((1, DOCS), f32)),
        in_specs=[pl.BlockSpec(memory_space=pl.ANY)] * 2,
        out_specs=(vmem, vmem),
        scratch_shapes=[
            pltpu.VMEM((DOCS, WIDTH), bf16),
            pltpu.VMEM((WIDTH, DOCS), bf16),
            pltpu.VMEM((ROWS, WIDTH), f32),
            pltpu.VMEM((4, HALF, WIDTH), bf16),
            pltpu.VMEM((4, HALF, WIDTH), bf16),
            pltpu.VMEM((4, 2 * HALF, DOCS), bf16),
            pltpu.VMEM((GROUPS, DOCS), f32),
            pltpu.VMEM((GROUPS, DOCS), f32),
            pltpu.VMEM((8, 1, DOCS), f32),
            pltpu.VMEM((GROUPS, DOCS), f32),
            pltpu.VMEM((HALF, WIDE), f32),
            pltpu.VMEM((4, 1, TALL, 128), f32),
            pltpu.VMEM((4, HALF, WIDE), bf16),
            pltpu.VMEM((4, HALF, WIDE), bf16),
            pltpu.VMEM((4, 4, TALL, 128), bf16),
            pltpu.VMEM((4, 3, TALL, 128), bf16),
            pltpu.VMEM((3, TALL, 128), bf16),
            pltpu.VMEM((3, TALL, 128), bf16),
            dma, dma, flag, flag,
            dma((4,)), dma((4,)),
            dma((4, 4)), dma((4, 4)),
            dma((4, 4)), dma((4, 4)),
            dma((8,)), dma((8,)),
            dma((5,)), dma((5,)),
            dma((5, 4)), dma((5, 4)),
            dma((4,)), dma((4,)),
        ],
        compiler_params=pltpu.CompilerParams(
            collective_id=0, has_side_effects=True, vmem_limit_bytes=52 * 2**20
        ),
        cost_estimate=pl.CostEstimate(
            flops=4 * DOCS * WIDTH * 1024, bytes_accessed=2 * DOCS * WIDTH, transcendentals=DOCS * 1024
        ),
        name="em_step",
    )(docs, centroids)
    return pl.pallas_call(
        finish_kernel,
        out_shape=(
            jax.ShapeDtypeStruct((ROWS, WIDTH), f32),
            jax.ShapeDtypeStruct((ROWS,), f32),
            jax.ShapeDtypeStruct((DOCS,), f32),
        ),
        in_specs=[vmem] * 3,
        out_specs=(vmem,) * 3,
        compiler_params=pltpu.CompilerParams(vmem_limit_bytes=8 * 2**20),
        name="finish",
    )(acc, lse, centroids)


def solution(mesh):
    in_specs = (P("dev", None), P(("cgrp", "dev"), None))
    out_specs = (P(("cgrp", "dev"), None), P(("cgrp", "dev")), P("dev"))
    return jax.shard_map(body, mesh=mesh, in_specs=in_specs, out_specs=out_specs, check_vma=False)
```

```python
import jax
import jax.numpy as jnp
from jax import lax
from jax.experimental import pallas as pl
from jax.experimental.pallas import tpu as pltpu
from jax.sharding import PartitionSpec as P

MESH = pl.DeviceIdType.MESH
WIDTH = 1024
DOCS = 2048
ROWS = 32
HALF = 128
WIDE = WIDTH + 128
LINES = ROWS * WIDTH // 128
TALL = LINES + 16
SCALE = 0.125
TILE = 256
GROUPS = 10


def em_kernel(
    docs_hbm, cent_hbm, acc_ref, mass_ref, lse_ref,
    docs, turned, cent, mine, sib, expo, top, total, lses, factor,
    keep, keep_own, out_sib, in_sib, out_v, in_v, out_a, in_a,
    docs_sem, cent_sem, low_sem, high_sem,
    s1, r1, s2, r2, s3, r3, s4, r4, s5, r5, s6, r6, s7, r7,
):
    z = lax.axis_index("cgrp")
    dev = lax.axis_index("dev")
    core = lax.rem(dev, 2)
    x = lax.div(dev, 8)
    y = lax.rem(lax.div(dev, 2), 4)
    a = x * (1 - core) + y * core
    v = y * (1 - core) + x * core

    def at(da, dv):
        ai = lax.rem(a + (da + 4), 4)
        vi = lax.rem(v + (dv + 4), 4)
        xi = ai * (1 - core) + vi * core
        yi = vi * (1 - core) + ai * core
        return (z, (xi * 4 + yi) * 2 + core)

    sibling = (z, dev + 1 - 2 * core)

    def up(k):
        return (lax.rem(z + k, 8), dev)

    def rows(i, n=1):
        return pl.ds(i * ROWS, n * ROWS)

    def remote(src, dst, send, recv, where):
        return pltpu.make_async_remote_copy(
            src_ref=src, dst_ref=dst, send_sem=send, recv_sem=recv, device_id=where, device_id_type=MESH
        )

    def signal(sem, where):
        pl.semaphore_signal(sem, inc=1, device_id=where, device_id_type=MESH)

    barrier = pltpu.get_barrier_semaphore()
    greet = [at(0, 2), at(2, 0), at(0, 1), at(0, 3), at(1, 0), at(3, 0), sibling, up(1), up(7)]
    own = pltpu.make_async_copy(cent_hbm, cent, cent_sem)
    own.start()
    for where in greet:
        signal(barrier, where)
    load = pltpu.make_async_copy(docs_hbm, docs, docs_sem)
    load.start()
    own.wait()
    mine[0, rows(0)] = cent[...].astype(jnp.bfloat16)
    pl.semaphore_wait(barrier, len(greet))

    def tell_low():
        signal(low_sem, up(1))

    def tell_high():
        signal(high_sem, up(7))

    def told():
        pl.semaphore_wait(low_sem, 1)
        pl.semaphore_wait(high_sem, 1)

    def along_v(dv):
        return remote(mine.at[0, rows(0)], mine.at[0, rows(dv)], s1.at[dv], r1.at[dv], at(0, dv))

    def along_a(da, dj):
        return remote(mine.at[0, rows(dj)], mine.at[da, rows(dj)], s2.at[da, dj], r2.at[da, dj], at(da, 0))

    def across(da, dj):
        return remote(mine.at[da, rows(dj)], sib.at[da, rows(dj)], s3.at[da, dj], r3.at[da, dj], sibling)

    def scores(g, blocks):
        c = jnp.concatenate([b[t, rows(j, n)] for b, t, j, n, _ in blocks], axis=0)
        wide = c.astype(jnp.float32)
        bias = jnp.sum(wide * wide, axis=1, keepdims=True) * (0.5 * SCALE)
        for i in range(DOCS // TILE):
            part = pl.ds(i * TILE, TILE)
            dots = jnp.dot(c, turned[:, part], preferred_element_type=jnp.float32)
            s = dots * SCALE - bias
            m = jnp.max(s, axis=0, keepdims=True)
            p = jnp.exp(s - m)
            e = p.astype(jnp.bfloat16)
            done = 0
            for _, t, _, n, r in blocks:
                expo[t, rows(r, n), part] = e[done * ROWS:(done + n) * ROWS]
                done += n
            top[pl.ds(g, 1), part] = m
            total[pl.ds(g, 1), part] = jnp.sum(p, axis=0, keepdims=True)

    def from_mine(dj):
        return [(mine, da, dj, 1, dj) for da in (1, 2, 3)]

    def from_sib(dj):
        return [(sib, da, dj, 1, dj + 4) for da in (1, 2, 3)]

    def forward_a(dj):
        for da in (1, 3, 2):
            along_a(da, dj).wait_recv()
            across(da, dj).start()

    def wait_across(dj):
        for da in (1, 3, 2):
            across(da, dj).wait_recv()

    def turn(tiles):
        for i in tiles:
            part = pl.ds(i * TILE, TILE)
            turned[:, part] = jnp.transpose(docs[part, :])

    for k in (1, 3, 2):
        along_v(k).start()
    across(0, 0).start()
    tell_low()
    tell_high()
    for k in (1, 3, 2):
        along_a(k, 0).start()
    load.wait()
    turn(range(8))
    for dv in (1, 3, 2):
        along_v(dv).wait_recv()
        for da in (1, 3, 2):
            along_a(da, dv).start()
        across(0, dv).start()
    forward_a(0)
    told()
    tell_low()
    tell_high()
    scores(0, [(mine, 0, 0, 4, 0)])
    scores(1, from_mine(0))
    for dj in (0, 1, 3, 2):
        across(0, dj).wait_recv()
    scores(2, [(sib, 0, 0, 4, 4)])
    told()
    tell_low()
    wait_across(0)
    scores(3, from_sib(0))
    forward_a(1)
    scores(4, from_mine(1))
    forward_a(3)
    wait_across(1)
    scores(5, from_sib(1))
    scores(6, from_mine(3))
    forward_a(2)
    wait_across(3)
    scores(7, from_sib(3))
    scores(8, from_mine(2))
    wait_across(2)
    scores(9, from_sib(2))

    tops = top[...]
    m = jnp.max(tops, axis=0, keepdims=True)
    l = jnp.sum(total[...] * jnp.exp(tops - m), axis=0, keepdims=True)
    lses[z] = m + jnp.log(l)

    def along_z(k):
        return remote(lses.at[z], lses.at[z], s4.at[k], r4.at[k], up(k))

    def arrived_z(k):
        where = lses.at[lax.rem(z + 8 - k, 8)]
        return remote(where, where, s4.at[k], r4.at[k], up(k))

    pl.semaphore_wait(low_sem, 1)
    for k in (4, 3, 5, 2, 6, 1, 7):
        along_z(k).start()
    for dv in (1, 2, 3):
        along_v(dv).wait_send()
    for da in (1, 2, 3):
        for dj in range(4):
            along_a(da, dj).wait_send()
    for da in range(4):
        for dj in range(4):
            across(da, dj).wait_send()
    for k in (1, 7, 2, 6, 3, 5, 4):
        arrived_z(k).wait_recv()
    m = lses[0]
    for k in range(1, 8):
        m = jnp.maximum(m, lses[k])
    lse = m + jnp.log(sum(jnp.exp(lses[k] - m) for k in range(8)))
    lse_ref[...] = lse
    factor[...] = jnp.exp(tops - lse)

    pieces = {t: [(t, 0, WIDE, 0, TALL)] for t in range(4)}

    def give(t, piece):
        sem, col, n, _, _ = piece
        part = pl.ds(col, n)
        return remote(out_sib.at[t, :, part], in_sib.at[t, :, part], s5.at[sem], r5.at[sem], sibling)

    def sum_v(t, piece, dv):
        sem, _, _, first, n = piece
        part = pl.ds(first, n)
        return remote(
            out_v.at[t, 4 - dv, part], in_v.at[t, dv - 1, part], s6.at[sem, dv], r6.at[sem, dv], at(0, dv)
        )

    def sum_a(t):
        return remote(out_a.at[t - 1], in_a.at[t - 1], s7.at[t], r7.at[t], at(-t, 0))

    left = lax.broadcasted_iota(jnp.int32, (16, 128), 1) < 64

    def emit(t, col, both):
        for dj in (2, 3, 1, 0):
            block = both[dj * ROWS:(dj + 1) * ROWS]
            out = keep_own if dj == 0 else out_v
            for j in range(0, both.shape[1], 128):
                values = block[:, j:j + 128]
                if col + j == WIDTH:
                    values = jnp.where(left, values[:16], values[16:])
                lines = pl.ds((col + j) // 128 * ROWS, values.shape[0])
                out[t, dj, lines, :] = values.astype(out.dtype)

    def weigh(t, other, save, done):
        parts = [
            expo[t, rows(4 * other + dj)].astype(jnp.float32) * factor[pl.ds(first + step * other, 1), :]
            for dj, (first, step) in enumerate([(0, 2)] * 4 if t == 0 else [(1, 2), (4, 1), (8, 1), (6, 1)])
        ]
        resp = jnp.concatenate(parts, axis=0)
        mass = jnp.sum(resp, axis=1, keepdims=True)
        resp = resp.astype(jnp.bfloat16)
        for piece in pieces[t]:
            _, col, n, _, _ = piece
            for j in range(col, col + n, TILE):
                if j == WIDTH:
                    save(j, jnp.broadcast_to(mass, (HALF, 128)))
                else:
                    save(j, jnp.dot(resp, docs[:, pl.ds(j, TILE)], preferred_element_type=jnp.float32))
            done(piece)

    def theirs(t):
        def save(j, term):
            out_sib[t, :, pl.ds(j, term.shape[1])] = term.astype(jnp.bfloat16)

        weigh(t, 1, save, lambda piece: give(t, piece).start())

    def send_v(t, piece):
        for dv in (2, 1, 3):
            sum_v(t, piece, dv).start()

    def ours(t):
        for piece in pieces[t]:
            give(t, piece).wait_recv()

        def save(j, term):
            emit(t, j, term + in_sib[t, :, pl.ds(j, term.shape[1])].astype(jnp.float32))

        weigh(t, 0, save, lambda piece: send_v(t, piece))

    def ours_first(t):
        def save(j, term):
            keep[:, pl.ds(j, term.shape[1])] = term

        weigh(t, 0, save, lambda piece: None)
        for piece in pieces[t]:
            _, col, n, _, _ = piece
            give(t, piece).wait_recv()
            emit(t, col, keep[:, pl.ds(col, n)] + in_sib[t, :, pl.ds(col, n)].astype(jnp.float32))
            send_v(t, piece)

    def row(t):
        for piece in pieces[t]:
            for dv in (1, 3, 2):
                sum_v(t, piece, dv).wait_recv()
        own = keep_own[t, 0]
        for dv in (1, 2, 3):
            own = own + in_v[t, dv - 1].astype(jnp.float32)
        if t == 0:
            return own
        out_a[t - 1] = own.astype(jnp.bfloat16)
        sum_a(t).start()

    theirs(2)
    theirs(1)
    ours_first(2)
    theirs(3)
    ours(1)
    theirs(0)
    ours(3)
    ours(0)
    for k in range(1, 8):
        along_z(k).wait_send()
    for t in range(4):
        for piece in pieces[t]:
            give(t, piece).wait_send()
    row(2)
    row(1)
    row(3)
    for t in (2, 1, 3):
        for dv in (1, 2, 3):
            for piece in pieces[t]:
                sum_v(t, piece, dv).wait_send()
    acc = row(0)
    for t in (1, 3, 2):
        sum_a(t).wait_recv()
        acc = acc + in_a[t - 1].astype(jnp.float32)
    acc_ref[...] = acc[:LINES].astype(jnp.bfloat16)
    mass_ref[...] = acc[LINES:]

    for t in (1, 2, 3):
        sum_a(t).wait_send()
    for dv in (1, 2, 3):
        sum_v(0, pieces[0][0], dv).wait_send()


def finish_kernel(acc_ref, packed_ref, lse_in, cent_ref, next_ref, mass_ref, lse_ref):
    packed = packed_ref[...]
    mass = jnp.concatenate([packed[:, :1], packed[:, 64:65]], axis=0)
    for j in range(WIDTH // 128):
        part = pl.ds(j * 128, 128)
        next_ref[:, part] = (acc_ref[pl.ds(j * ROWS, ROWS), :].astype(jnp.float32) + cent_ref[:, part]) / (mass + 1.0)
    mass_ref[...] = jnp.transpose(jnp.broadcast_to(mass, (ROWS, 128)))[0]
    lse_ref[...] = lse_in[0]


def body(docs, centroids):
    bf16, f32 = jnp.bfloat16, jnp.float32
    dma = pltpu.SemaphoreType.DMA
    flag = pltpu.SemaphoreType.REGULAR
    vmem = pl.BlockSpec(memory_space=pltpu.VMEM)
    acc, packed, lse = pl.pallas_call(
        em_kernel,
        out_shape=(
            jax.ShapeDtypeStruct((LINES, 128), bf16),
            jax.ShapeDtypeStruct((16, 128), f32),
            jax.ShapeDtypeStruct((1, DOCS), f32),
        ),
        in_specs=[pl.BlockSpec(memory_space=pl.ANY)] * 2,
        out_specs=(vmem,) * 3,
        scratch_shapes=[
            pltpu.VMEM((DOCS, WIDTH), bf16),
            pltpu.VMEM((WIDTH, DOCS), bf16),
            pltpu.VMEM((ROWS, WIDTH), f32),
            pltpu.VMEM((4, HALF, WIDTH), bf16),
            pltpu.VMEM((4, HALF, WIDTH), bf16),
            pltpu.VMEM((4, 2 * HALF, DOCS), bf16),
            pltpu.VMEM((GROUPS, DOCS), f32),
            pltpu.VMEM((GROUPS, DOCS), f32),
            pltpu.VMEM((8, 1, DOCS), f32),
            pltpu.VMEM((GROUPS, DOCS), f32),
            pltpu.VMEM((HALF, WIDE), f32),
            pltpu.VMEM((4, 1, TALL, 128), f32),
            pltpu.VMEM((4, HALF, WIDE), bf16),
            pltpu.VMEM((4, HALF, WIDE), bf16),
            pltpu.VMEM((4, 4, TALL, 128), bf16),
            pltpu.VMEM((4, 3, TALL, 128), bf16),
            pltpu.VMEM((3, TALL, 128), bf16),
            pltpu.VMEM((3, TALL, 128), bf16),
            dma, dma, flag, flag,
            dma((4,)), dma((4,)),
            dma((4, 4)), dma((4, 4)),
            dma((4, 4)), dma((4, 4)),
            dma((8,)), dma((8,)),
            dma((5,)), dma((5,)),
            dma((5, 4)), dma((5, 4)),
            dma((4,)), dma((4,)),
        ],
        compiler_params=pltpu.CompilerParams(
            collective_id=0, has_side_effects=True, vmem_limit_bytes=55072 * 2**10
        ),
        cost_estimate=pl.CostEstimate(
            flops=4 * DOCS * WIDTH * 1024, bytes_accessed=2 * DOCS * WIDTH, transcendentals=DOCS * 1024
        ),
        name="em_step",
    )(docs, centroids)
    return pl.pallas_call(
        finish_kernel,
        out_shape=(
            jax.ShapeDtypeStruct((ROWS, WIDTH), f32),
            jax.ShapeDtypeStruct((ROWS,), f32),
            jax.ShapeDtypeStruct((DOCS,), f32),
        ),
        in_specs=[vmem] * 4,
        out_specs=(vmem,) * 3,
        compiler_params=pltpu.CompilerParams(vmem_limit_bytes=8 * 2**20),
        name="finish",
    )(acc, packed, lse, centroids)


def solution(mesh):
    in_specs = (P("dev", None), P(("cgrp", "dev"), None))
    out_specs = (P(("cgrp", "dev"), None), P(("cgrp", "dev")), P("dev"))
    return jax.shard_map(body, mesh=mesh, in_specs=in_specs, out_specs=out_specs, check_vma=False)
```

```python
import jax
import jax.numpy as jnp
from jax import lax
from jax.experimental import pallas as pl
from jax.experimental.pallas import tpu as pltpu
from jax.sharding import PartitionSpec as P

MESH = pl.DeviceIdType.MESH
WIDTH = 1024
DOCS = 2048
ROWS = 32
HALF = 128
WIDE = WIDTH + 128
LINES = ROWS * WIDTH // 128
TALL = LINES + 16
SCALE = 0.125
TILE = 256
GROUPS = 8


def em_kernel(
    docs_hbm, cent_hbm, acc_ref, mass_ref, lse_ref,
    docs, turned, cent, mine, sib, expo, top, total, lses, factor,
    keep, keep_own, out_sib, in_sib, out_v, in_v, out_a, in_a,
    docs_sem, cent_sem, low_sem, high_sem,
    s1, r1, s2, r2, s3, r3, s4, r4, s5, r5, s6, r6, s7, r7,
):
    z = lax.axis_index("cgrp")
    dev = lax.axis_index("dev")
    core = lax.rem(dev, 2)
    x = lax.div(dev, 8)
    y = lax.rem(lax.div(dev, 2), 4)
    a = x * (1 - core) + y * core
    v = y * (1 - core) + x * core

    def at(da, dv):
        ai = lax.rem(a + (da + 4), 4)
        vi = lax.rem(v + (dv + 4), 4)
        xi = ai * (1 - core) + vi * core
        yi = vi * (1 - core) + ai * core
        return (z, (xi * 4 + yi) * 2 + core)

    sibling = (z, dev + 1 - 2 * core)

    def up(k):
        return (lax.rem(z + k, 8), dev)

    def rows(i, n=1):
        return pl.ds(i * ROWS, n * ROWS)

    def remote(src, dst, send, recv, where):
        return pltpu.make_async_remote_copy(
            src_ref=src, dst_ref=dst, send_sem=send, recv_sem=recv, device_id=where, device_id_type=MESH
        )

    def signal(sem, where):
        pl.semaphore_signal(sem, inc=1, device_id=where, device_id_type=MESH)

    barrier = pltpu.get_barrier_semaphore()
    greet = [at(0, 2), at(2, 0), at(0, 1), at(0, 3), at(1, 0), at(3, 0), sibling, up(1), up(7)]
    own = pltpu.make_async_copy(cent_hbm, cent, cent_sem)
    own.start()
    for where in greet:
        signal(barrier, where)
    load = pltpu.make_async_copy(docs_hbm, docs, docs_sem)
    load.start()
    own.wait()
    mine[0, rows(0)] = cent[...].astype(jnp.bfloat16)
    pl.semaphore_wait(barrier, len(greet))

    def tell_low():
        signal(low_sem, up(1))

    def tell_high():
        signal(high_sem, up(7))

    def told():
        pl.semaphore_wait(low_sem, 1)
        pl.semaphore_wait(high_sem, 1)

    def along_v(dv):
        return remote(mine.at[0, rows(0)], mine.at[0, rows(dv)], s1.at[dv], r1.at[dv], at(0, dv))

    def along_a(da, dj):
        return remote(mine.at[0, rows(dj)], mine.at[da, rows(dj)], s2.at[da, dj], r2.at[da, dj], at(da, 0))

    def across(da, dj):
        return remote(mine.at[da, rows(dj)], sib.at[da, rows(dj)], s3.at[da, dj], r3.at[da, dj], sibling)

    def scores(g, blocks):
        c = jnp.concatenate([b[t, rows(j, n)] for b, t, j, n, _ in blocks], axis=0)
        wide = c.astype(jnp.float32)
        bias = jnp.sum(wide * wide, axis=1, keepdims=True) * (0.5 * SCALE)
        for i in range(DOCS // TILE):
            part = pl.ds(i * TILE, TILE)
            dots = jnp.dot(c, turned[:, part], preferred_element_type=jnp.float32)
            s = dots * SCALE - bias
            m = jnp.max(s, axis=0, keepdims=True)
            p = jnp.exp(s - m)
            e = p.astype(jnp.bfloat16)
            done = 0
            for _, t, _, n, r in blocks:
                expo[t, rows(r, n), part] = e[done * ROWS:(done + n) * ROWS]
                done += n
            top[pl.ds(g, 1), part] = m
            total[pl.ds(g, 1), part] = jnp.sum(p, axis=0, keepdims=True)

    def from_mine(dj):
        return [(mine, da, dj, 1, dj) for da in (1, 2, 3)]

    def from_sib(dj):
        return [(sib, da, dj, 1, dj + 4) for da in (1, 2, 3)]

    def forward_a(dj):
        for da in (1, 3, 2):
            along_a(da, dj).wait_recv()
            across(da, dj).start()

    def wait_across(dj):
        for da in (1, 3, 2):
            across(da, dj).wait_recv()

    def turn(tiles):
        for i in tiles:
            part = pl.ds(i * TILE, TILE)
            turned[:, part] = jnp.transpose(docs[part, :])

    for k in (1, 3, 2):
        along_v(k).start()
    across(0, 0).start()
    tell_low()
    tell_high()
    for k in (1, 3, 2):
        along_a(k, 0).start()
    load.wait()
    turn(range(8))
    for dv in (1, 3, 2):
        along_v(dv).wait_recv()
        for da in (1, 3, 2):
            along_a(da, dv).start()
        across(0, dv).start()
    forward_a(0)
    told()
    tell_low()
    tell_high()
    scores(0, [(mine, 0, 0, 4, 0)])
    scores(1, from_mine(0))
    for dj in (0, 1, 3, 2):
        across(0, dj).wait_recv()
    scores(2, [(sib, 0, 0, 4, 4)])
    told()
    tell_low()
    wait_across(0)
    scores(3, from_sib(0))
    forward_a(1)
    scores(4, from_mine(1))
    forward_a(3)
    wait_across(1)
    scores(5, from_sib(1) + from_mine(3))
    forward_a(2)
    wait_across(3)
    scores(6, from_sib(3) + from_mine(2))
    wait_across(2)
    scores(7, from_sib(2))

    tops = top[...]
    m = jnp.max(tops, axis=0, keepdims=True)
    l = jnp.sum(total[...] * jnp.exp(tops - m), axis=0, keepdims=True)
    lses[z] = m + jnp.log(l)

    def along_z(k):
        return remote(lses.at[z], lses.at[z], s4.at[k], r4.at[k], up(k))

    def arrived_z(k):
        where = lses.at[lax.rem(z + 8 - k, 8)]
        return remote(where, where, s4.at[k], r4.at[k], up(k))

    pl.semaphore_wait(low_sem, 1)
    for k in (4, 3, 5, 2, 6, 1, 7):
        along_z(k).start()
    for dv in (1, 2, 3):
        along_v(dv).wait_send()
    for da in (1, 2, 3):
        for dj in range(4):
            along_a(da, dj).wait_send()
    for da in range(4):
        for dj in range(4):
            across(da, dj).wait_send()
    for k in (1, 7, 2, 6, 3, 5, 4):
        arrived_z(k).wait_recv()
    m = lses[0]
    for k in range(1, 8):
        m = jnp.maximum(m, lses[k])
    lse = m + jnp.log(sum(jnp.exp(lses[k] - m) for k in range(8)))
    lse_ref[...] = lse
    factor[...] = jnp.exp(tops - lse)

    pieces = {t: [(t, 0, WIDE, 0, TALL)] for t in range(4)}

    def give(t, piece):
        sem, col, n, _, _ = piece
        part = pl.ds(col, n)
        return remote(out_sib.at[t, :, part], in_sib.at[t, :, part], s5.at[sem], r5.at[sem], sibling)

    def sum_v(t, piece, dv):
        sem, _, _, first, n = piece
        part = pl.ds(first, n)
        return remote(
            out_v.at[t, 4 - dv, part], in_v.at[t, dv - 1, part], s6.at[sem, dv], r6.at[sem, dv], at(0, dv)
        )

    def sum_a(t):
        return remote(out_a.at[t - 1], in_a.at[t - 1], s7.at[t], r7.at[t], at(-t, 0))

    left = lax.broadcasted_iota(jnp.int32, (16, 128), 1) < 64

    def emit(t, col, both):
        for dj in (2, 3, 1, 0):
            block = both[dj * ROWS:(dj + 1) * ROWS]
            out = keep_own if dj == 0 else out_v
            for j in range(0, both.shape[1], 128):
                values = block[:, j:j + 128]
                if col + j == WIDTH:
                    values = jnp.where(left, values[:16], values[16:])
                lines = pl.ds((col + j) // 128 * ROWS, values.shape[0])
                out[t, dj, lines, :] = values.astype(out.dtype)

    def weigh(t, other, save, done):
        parts = [
            expo[t, rows(4 * other + dj)].astype(jnp.float32) * factor[pl.ds(first + step * other, 1), :]
            for dj, (first, step) in enumerate([(0, 2)] * 4 if t == 0 else [(1, 2), (4, 1), (6, 1), (5, 1)])
        ]
        resp = jnp.concatenate(parts, axis=0)
        mass = jnp.sum(resp, axis=1, keepdims=True)
        resp = resp.astype(jnp.bfloat16)
        for piece in pieces[t]:
            _, col, n, _, _ = piece
            for j in range(col, col + n, TILE):
                if j == WIDTH:
                    save(j, jnp.broadcast_to(mass, (HALF, 128)))
                else:
                    save(j, jnp.dot(resp, docs[:, pl.ds(j, TILE)], preferred_element_type=jnp.float32))
            done(piece)

    def theirs(t):
        def save(j, term):
            out_sib[t, :, pl.ds(j, term.shape[1])] = term.astype(jnp.bfloat16)

        weigh(t, 1, save, lambda piece: give(t, piece).start())

    def send_v(t, piece):
        for dv in (2, 1, 3):
            sum_v(t, piece, dv).start()

    def ours(t):
        for piece in pieces[t]:
            give(t, piece).wait_recv()

        def save(j, term):
            emit(t, j, term + in_sib[t, :, pl.ds(j, term.shape[1])].astype(jnp.float32))

        weigh(t, 0, save, lambda piece: send_v(t, piece))

    def ours_first(t):
        def save(j, term):
            keep[:, pl.ds(j, term.shape[1])] = term

        weigh(t, 0, save, lambda piece: None)
        for piece in pieces[t]:
            _, col, n, _, _ = piece
            give(t, piece).wait_recv()
            emit(t, col, keep[:, pl.ds(col, n)] + in_sib[t, :, pl.ds(col, n)].astype(jnp.float32))
            send_v(t, piece)

    def row(t):
        for piece in pieces[t]:
            for dv in (1, 3, 2):
                sum_v(t, piece, dv).wait_recv()
        own = keep_own[t, 0]
        for dv in (1, 2, 3):
            own = own + in_v[t, dv - 1].astype(jnp.float32)
        if t == 0:
            return own
        out_a[t - 1] = own.astype(jnp.bfloat16)
        sum_a(t).start()

    theirs(2)
    theirs(1)
    ours_first(2)
    theirs(3)
    ours(1)
    theirs(0)
    ours(3)
    ours(0)
    for k in range(1, 8):
        along_z(k).wait_send()
    for t in range(4):
        for piece in pieces[t]:
            give(t, piece).wait_send()
    row(2)
    row(1)
    row(3)
    for t in (2, 1, 3):
        for dv in (1, 2, 3):
            for piece in pieces[t]:
                sum_v(t, piece, dv).wait_send()
    acc = row(0)
    for t in (1, 3, 2):
        sum_a(t).wait_recv()
        acc = acc + in_a[t - 1].astype(jnp.float32)
    acc_ref[...] = acc[:LINES].astype(jnp.bfloat16)
    mass_ref[...] = acc[LINES:]

    for t in (1, 2, 3):
        sum_a(t).wait_send()
    for dv in (1, 2, 3):
        sum_v(0, pieces[0][0], dv).wait_send()


def finish_kernel(acc_ref, packed_ref, lse_in, cent_ref, next_ref, mass_ref, lse_ref):
    packed = packed_ref[...]
    mass = jnp.concatenate([packed[:, :1], packed[:, 64:65]], axis=0)
    for j in range(WIDTH // 128):
        part = pl.ds(j * 128, 128)
        next_ref[:, part] = (acc_ref[pl.ds(j * ROWS, ROWS), :].astype(jnp.float32) + cent_ref[:, part]) / (mass + 1.0)
    mass_ref[...] = jnp.transpose(jnp.broadcast_to(mass, (ROWS, 128)))[0]
    lse_ref[...] = lse_in[0]


def body(docs, centroids):
    bf16, f32 = jnp.bfloat16, jnp.float32
    dma = pltpu.SemaphoreType.DMA
    flag = pltpu.SemaphoreType.REGULAR
    vmem = pl.BlockSpec(memory_space=pltpu.VMEM)
    acc, packed, lse = pl.pallas_call(
        em_kernel,
        out_shape=(
            jax.ShapeDtypeStruct((LINES, 128), bf16),
            jax.ShapeDtypeStruct((16, 128), f32),
            jax.ShapeDtypeStruct((1, DOCS), f32),
        ),
        in_specs=[pl.BlockSpec(memory_space=pl.ANY)] * 2,
        out_specs=(vmem,) * 3,
        scratch_shapes=[
            pltpu.VMEM((DOCS, WIDTH), bf16),
            pltpu.VMEM((WIDTH, DOCS), bf16),
            pltpu.VMEM((ROWS, WIDTH), f32),
            pltpu.VMEM((4, HALF, WIDTH), bf16),
            pltpu.VMEM((4, HALF, WIDTH), bf16),
            pltpu.VMEM((4, 2 * HALF, DOCS), bf16),
            pltpu.VMEM((GROUPS, DOCS), f32),
            pltpu.VMEM((GROUPS, DOCS), f32),
            pltpu.VMEM((8, 1, DOCS), f32),
            pltpu.VMEM((GROUPS, DOCS), f32),
            pltpu.VMEM((HALF, WIDE), f32),
            pltpu.VMEM((4, 1, TALL, 128), f32),
            pltpu.VMEM((4, HALF, WIDE), bf16),
            pltpu.VMEM((4, HALF, WIDE), bf16),
            pltpu.VMEM((4, 4, TALL, 128), bf16),
            pltpu.VMEM((4, 3, TALL, 128), bf16),
            pltpu.VMEM((3, TALL, 128), bf16),
            pltpu.VMEM((3, TALL, 128), bf16),
            dma, dma, flag, flag,
            dma((4,)), dma((4,)),
            dma((4, 4)), dma((4, 4)),
            dma((4, 4)), dma((4, 4)),
            dma((8,)), dma((8,)),
            dma((5,)), dma((5,)),
            dma((5, 4)), dma((5, 4)),
            dma((4,)), dma((4,)),
        ],
        compiler_params=pltpu.CompilerParams(
            collective_id=0, has_side_effects=True, vmem_limit_bytes=55072 * 2**10
        ),
        cost_estimate=pl.CostEstimate(
            flops=4 * DOCS * WIDTH * 1024, bytes_accessed=2 * DOCS * WIDTH, transcendentals=DOCS * 1024
        ),
        name="em_step",
    )(docs, centroids)
    return pl.pallas_call(
        finish_kernel,
        out_shape=(
            jax.ShapeDtypeStruct((ROWS, WIDTH), f32),
            jax.ShapeDtypeStruct((ROWS,), f32),
            jax.ShapeDtypeStruct((DOCS,), f32),
        ),
        in_specs=[vmem] * 4,
        out_specs=(vmem,) * 3,
        compiler_params=pltpu.CompilerParams(vmem_limit_bytes=8 * 2**20),
        name="finish",
    )(acc, packed, lse, centroids)


def solution(mesh):
    in_specs = (P("dev", None), P(("cgrp", "dev"), None))
    out_specs = (P(("cgrp", "dev"), None), P(("cgrp", "dev")), P("dev"))
    return jax.shard_map(body, mesh=mesh, in_specs=in_specs, out_specs=out_specs, check_vma=False)
```

```python
import jax
import jax.numpy as jnp
from jax import lax
from jax.experimental import pallas as pl
from jax.experimental.pallas import tpu as pltpu
from jax.sharding import PartitionSpec as P

MESH = pl.DeviceIdType.MESH
WIDTH = 1024
DOCS = 2048
ROWS = 32
HALF = 128
WIDE = WIDTH + 128
LINES = ROWS * WIDTH // 128
TALL = LINES + 16
SCALE = 0.125
TILE = 256
GROUPS = 7


def em_kernel(
    docs_hbm, cent_hbm, acc_ref, mass_ref, lse_ref,
    docs, turned, cent, mine, sib, expo, top, total, lses, factor,
    keep, keep_own, out_sib, in_sib, out_v, in_v, out_a, in_a,
    docs_sem, cent_sem, low_sem, high_sem,
    s1, r1, s2, r2, s3, r3, s4, r4, s5, r5, s6, r6, s7, r7,
):
    z = lax.axis_index("cgrp")
    dev = lax.axis_index("dev")
    core = lax.rem(dev, 2)
    x = lax.div(dev, 8)
    y = lax.rem(lax.div(dev, 2), 4)
    a = x * (1 - core) + y * core
    v = y * (1 - core) + x * core

    def at(da, dv):
        ai = lax.rem(a + (da + 4), 4)
        vi = lax.rem(v + (dv + 4), 4)
        xi = ai * (1 - core) + vi * core
        yi = vi * (1 - core) + ai * core
        return (z, (xi * 4 + yi) * 2 + core)

    sibling = (z, dev + 1 - 2 * core)

    def up(k):
        return (lax.rem(z + k, 8), dev)

    def rows(i, n=1):
        return pl.ds(i * ROWS, n * ROWS)

    def remote(src, dst, send, recv, where):
        return pltpu.make_async_remote_copy(
            src_ref=src, dst_ref=dst, send_sem=send, recv_sem=recv, device_id=where, device_id_type=MESH
        )

    def signal(sem, where):
        pl.semaphore_signal(sem, inc=1, device_id=where, device_id_type=MESH)

    barrier = pltpu.get_barrier_semaphore()
    greet = [at(0, 2), at(2, 0), at(0, 1), at(0, 3), at(1, 0), at(3, 0), sibling, up(1), up(7)]
    own = pltpu.make_async_copy(cent_hbm, cent, cent_sem)
    own.start()
    for where in greet:
        signal(barrier, where)
    load = pltpu.make_async_copy(docs_hbm, docs, docs_sem)
    load.start()
    own.wait()
    mine[0, rows(0)] = cent[...].astype(jnp.bfloat16)
    pl.semaphore_wait(barrier, len(greet))

    def tell_low():
        signal(low_sem, up(1))

    def tell_high():
        signal(high_sem, up(7))

    def told():
        pl.semaphore_wait(low_sem, 1)
        pl.semaphore_wait(high_sem, 1)

    def along_v(dv):
        return remote(mine.at[0, rows(0)], mine.at[0, rows(dv)], s1.at[dv], r1.at[dv], at(0, dv))

    def along_a(da, dj):
        return remote(mine.at[0, rows(dj)], mine.at[da, rows(dj)], s2.at[da, dj], r2.at[da, dj], at(da, 0))

    def across(da, dj):
        return remote(mine.at[da, rows(dj)], sib.at[da, rows(dj)], s3.at[da, dj], r3.at[da, dj], sibling)

    def scores(g, blocks):
        c = jnp.concatenate([b[t, rows(j, n)] for b, t, j, n, _ in blocks], axis=0)
        wide = c.astype(jnp.float32)
        bias = jnp.sum(wide * wide, axis=1, keepdims=True) * (0.5 * SCALE)
        for i in range(DOCS // TILE):
            part = pl.ds(i * TILE, TILE)
            dots = jnp.dot(c, turned[:, part], preferred_element_type=jnp.float32)
            s = dots * SCALE - bias
            m = jnp.max(s, axis=0, keepdims=True)
            p = jnp.exp(s - m)
            e = p.astype(jnp.bfloat16)
            done = 0
            for _, t, _, n, r in blocks:
                expo[t, rows(r, n), part] = e[done * ROWS:(done + n) * ROWS]
                done += n
            top[pl.ds(g, 1), part] = m
            total[pl.ds(g, 1), part] = jnp.sum(p, axis=0, keepdims=True)

    def from_mine(dj):
        return [(mine, da, dj, 1, dj) for da in (1, 2, 3)]

    def from_sib(dj):
        return [(sib, da, dj, 1, dj + 4) for da in (1, 2, 3)]

    def forward_a(dj):
        for da in (1, 3, 2):
            along_a(da, dj).wait_recv()
            across(da, dj).start()

    def wait_across(dj):
        for da in (1, 3, 2):
            across(da, dj).wait_recv()

    def turn(tiles):
        for i in tiles:
            part = pl.ds(i * TILE, TILE)
            turned[:, part] = jnp.transpose(docs[part, :])

    for k in (1, 3, 2):
        along_v(k).start()
    across(0, 0).start()
    tell_low()
    tell_high()
    for k in (1, 3, 2):
        along_a(k, 0).start()
    load.wait()
    turn(range(8))
    for dv in (1, 3, 2):
        along_v(dv).wait_recv()
        for da in (1, 3, 2):
            along_a(da, dv).start()
        across(0, dv).start()
    forward_a(0)
    told()
    tell_low()
    tell_high()
    scores(0, [(mine, 0, 0, 4, 0)])
    scores(1, from_mine(0))
    for dj in (0, 1, 3, 2):
        across(0, dj).wait_recv()
    scores(2, [(sib, 0, 0, 4, 4)])
    told()
    tell_low()
    wait_across(0)
    forward_a(1)
    scores(3, from_sib(0) + from_mine(1))
    forward_a(3)
    wait_across(1)
    scores(4, from_sib(1) + from_mine(3))
    forward_a(2)
    wait_across(3)
    scores(5, from_sib(3) + from_mine(2))
    wait_across(2)
    scores(6, from_sib(2))

    tops = top[...]
    m = jnp.max(tops, axis=0, keepdims=True)
    l = jnp.sum(total[...] * jnp.exp(tops - m), axis=0, keepdims=True)
    lses[z] = m + jnp.log(l)

    def along_z(k):
        return remote(lses.at[z], lses.at[z], s4.at[k], r4.at[k], up(k))

    def arrived_z(k):
        where = lses.at[lax.rem(z + 8 - k, 8)]
        return remote(where, where, s4.at[k], r4.at[k], up(k))

    pl.semaphore_wait(low_sem, 1)
    for k in (4, 3, 5, 2, 6, 1, 7):
        along_z(k).start()
    for dv in (1, 2, 3):
        along_v(dv).wait_send()
    for da in (1, 2, 3):
        for dj in range(4):
            along_a(da, dj).wait_send()
    for da in range(4):
        for dj in range(4):
            across(da, dj).wait_send()
    for k in (1, 7, 2, 6, 3, 5, 4):
        arrived_z(k).wait_recv()
    m = lses[0]
    for k in range(1, 8):
        m = jnp.maximum(m, lses[k])
    lse = m + jnp.log(sum(jnp.exp(lses[k] - m) for k in range(8)))
    lse_ref[...] = lse
    factor[...] = jnp.exp(tops - lse)

    pieces = {t: [(t, 0, WIDE, 0, TALL)] for t in range(4)}

    def give(t, piece):
        sem, col, n, _, _ = piece
        part = pl.ds(col, n)
        return remote(out_sib.at[t, :, part], in_sib.at[t, :, part], s5.at[sem], r5.at[sem], sibling)

    def sum_v(t, piece, dv):
        sem, _, _, first, n = piece
        part = pl.ds(first, n)
        return remote(
            out_v.at[t, 4 - dv, part], in_v.at[t, dv - 1, part], s6.at[sem, dv], r6.at[sem, dv], at(0, dv)
        )

    def sum_a(t):
        return remote(out_a.at[t - 1], in_a.at[t - 1], s7.at[t], r7.at[t], at(-t, 0))

    left = lax.broadcasted_iota(jnp.int32, (16, 128), 1) < 64

    def emit(t, col, both):
        for dj in (2, 3, 1, 0):
            block = both[dj * ROWS:(dj + 1) * ROWS]
            out = keep_own if dj == 0 else out_v
            for j in range(0, both.shape[1], 128):
                values = block[:, j:j + 128]
                if col + j == WIDTH:
                    values = jnp.where(left, values[:16], values[16:])
                lines = pl.ds((col + j) // 128 * ROWS, values.shape[0])
                out[t, dj, lines, :] = values.astype(out.dtype)

    def weigh(t, other, save, done):
        parts = [
            expo[t, rows(4 * other + dj)].astype(jnp.float32) * factor[pl.ds(first + step * other, 1), :]
            for dj, (first, step) in enumerate([(0, 2)] * 4 if t == 0 else [(1, 2), (3, 1), (5, 1), (4, 1)])
        ]
        resp = jnp.concatenate(parts, axis=0)
        mass = jnp.sum(resp, axis=1, keepdims=True)
        resp = resp.astype(jnp.bfloat16)
        for piece in pieces[t]:
            _, col, n, _, _ = piece
            for j in range(col, col + n, TILE):
                if j == WIDTH:
                    save(j, jnp.broadcast_to(mass, (HALF, 128)))
                else:
                    save(j, jnp.dot(resp, docs[:, pl.ds(j, TILE)], preferred_element_type=jnp.float32))
            done(piece)

    def theirs(t):
        def save(j, term):
            out_sib[t, :, pl.ds(j, term.shape[1])] = term.astype(jnp.bfloat16)

        weigh(t, 1, save, lambda piece: give(t, piece).start())

    def send_v(t, piece):
        for dv in (2, 1, 3):
            sum_v(t, piece, dv).start()

    def ours(t):
        for piece in pieces[t]:
            give(t, piece).wait_recv()

        def save(j, term):
            emit(t, j, term + in_sib[t, :, pl.ds(j, term.shape[1])].astype(jnp.float32))

        weigh(t, 0, save, lambda piece: send_v(t, piece))

    def ours_first(t):
        def save(j, term):
            keep[:, pl.ds(j, term.shape[1])] = term

        weigh(t, 0, save, lambda piece: None)
        for piece in pieces[t]:
            _, col, n, _, _ = piece
            give(t, piece).wait_recv()
            emit(t, col, keep[:, pl.ds(col, n)] + in_sib[t, :, pl.ds(col, n)].astype(jnp.float32))
            send_v(t, piece)

    def row(t):
        for piece in pieces[t]:
            for dv in (1, 3, 2):
                sum_v(t, piece, dv).wait_recv()
        own = keep_own[t, 0]
        for dv in (1, 2, 3):
            own = own + in_v[t, dv - 1].astype(jnp.float32)
        if t == 0:
            return own
        out_a[t - 1] = own.astype(jnp.bfloat16)
        sum_a(t).start()

    theirs(2)
    theirs(1)
    ours_first(2)
    theirs(3)
    ours(1)
    theirs(0)
    ours(3)
    ours(0)
    for k in range(1, 8):
        along_z(k).wait_send()
    for t in range(4):
        for piece in pieces[t]:
            give(t, piece).wait_send()
    row(2)
    row(1)
    row(3)
    for t in (2, 1, 3):
        for dv in (1, 2, 3):
            for piece in pieces[t]:
                sum_v(t, piece, dv).wait_send()
    acc = row(0)
    for t in (1, 3, 2):
        sum_a(t).wait_recv()
        acc = acc + in_a[t - 1].astype(jnp.float32)
    acc_ref[...] = acc[:LINES].astype(jnp.bfloat16)
    mass_ref[...] = acc[LINES:]

    for t in (1, 2, 3):
        sum_a(t).wait_send()
    for dv in (1, 2, 3):
        sum_v(0, pieces[0][0], dv).wait_send()


def finish_kernel(acc_ref, packed_ref, lse_in, cent_ref, next_ref, mass_ref, lse_ref):
    packed = packed_ref[...]
    mass = jnp.concatenate([packed[:, :1], packed[:, 64:65]], axis=0)
    for j in range(WIDTH // 128):
        part = pl.ds(j * 128, 128)
        next_ref[:, part] = (acc_ref[pl.ds(j * ROWS, ROWS), :].astype(jnp.float32) + cent_ref[:, part]) / (mass + 1.0)
    mass_ref[...] = jnp.transpose(jnp.broadcast_to(mass, (ROWS, 128)))[0]
    lse_ref[...] = lse_in[0]


def body(docs, centroids):
    bf16, f32 = jnp.bfloat16, jnp.float32
    dma = pltpu.SemaphoreType.DMA
    flag = pltpu.SemaphoreType.REGULAR
    vmem = pl.BlockSpec(memory_space=pltpu.VMEM)
    acc, packed, lse = pl.pallas_call(
        em_kernel,
        out_shape=(
            jax.ShapeDtypeStruct((LINES, 128), bf16),
            jax.ShapeDtypeStruct((16, 128), f32),
            jax.ShapeDtypeStruct((1, DOCS), f32),
        ),
        in_specs=[pl.BlockSpec(memory_space=pl.ANY)] * 2,
        out_specs=(vmem,) * 3,
        scratch_shapes=[
            pltpu.VMEM((DOCS, WIDTH), bf16),
            pltpu.VMEM((WIDTH, DOCS), bf16),
            pltpu.VMEM((ROWS, WIDTH), f32),
            pltpu.VMEM((4, HALF, WIDTH), bf16),
            pltpu.VMEM((4, HALF, WIDTH), bf16),
            pltpu.VMEM((4, 2 * HALF, DOCS), bf16),
            pltpu.VMEM((GROUPS, DOCS), f32),
            pltpu.VMEM((GROUPS, DOCS), f32),
            pltpu.VMEM((8, 1, DOCS), f32),
            pltpu.VMEM((GROUPS, DOCS), f32),
            pltpu.VMEM((HALF, WIDE), f32),
            pltpu.VMEM((4, 1, TALL, 128), f32),
            pltpu.VMEM((4, HALF, WIDE), bf16),
            pltpu.VMEM((4, HALF, WIDE), bf16),
            pltpu.VMEM((4, 4, TALL, 128), bf16),
            pltpu.VMEM((4, 3, TALL, 128), bf16),
            pltpu.VMEM((3, TALL, 128), bf16),
            pltpu.VMEM((3, TALL, 128), bf16),
            dma, dma, flag, flag,
            dma((4,)), dma((4,)),
            dma((4, 4)), dma((4, 4)),
            dma((4, 4)), dma((4, 4)),
            dma((8,)), dma((8,)),
            dma((5,)), dma((5,)),
            dma((5, 4)), dma((5, 4)),
            dma((4,)), dma((4,)),
        ],
        compiler_params=pltpu.CompilerParams(
            collective_id=0, has_side_effects=True, vmem_limit_bytes=55072 * 2**10
        ),
        cost_estimate=pl.CostEstimate(
            flops=4 * DOCS * WIDTH * 1024, bytes_accessed=2 * DOCS * WIDTH, transcendentals=DOCS * 1024
        ),
        name="em_step",
    )(docs, centroids)
    return pl.pallas_call(
        finish_kernel,
        out_shape=(
            jax.ShapeDtypeStruct((ROWS, WIDTH), f32),
            jax.ShapeDtypeStruct((ROWS,), f32),
            jax.ShapeDtypeStruct((DOCS,), f32),
        ),
        in_specs=[vmem] * 4,
        out_specs=(vmem,) * 3,
        compiler_params=pltpu.CompilerParams(vmem_limit_bytes=8 * 2**20),
        name="finish",
    )(acc, packed, lse, centroids)


def solution(mesh):
    in_specs = (P("dev", None), P(("cgrp", "dev"), None))
    out_specs = (P(("cgrp", "dev"), None), P(("cgrp", "dev")), P("dev"))
    return jax.shard_map(body, mesh=mesh, in_specs=in_specs, out_specs=out_specs, check_vma=False)
```
